512 devices in a mesh: member: 4 (over y), lat: 8 (over x, core), lon: 16 (over z).
Axes of the slice: x: 4, y: 4, z: 16, core: 2. Of those that a mesh axis runs over, the one named last changes fastest.
Arguments:
- ice_flux: float32 [32, 256, 8, 512], P(('member', 'lat'), 'lon'), parts along dimension 0, may hold values from 0.5 to 1.5
- ice_frac: float32 [32, 256, 512], P(('member', 'lat'), 'lon'), parts along dimension 0, may hold values from 0.05 to 1
- ice_mask: int32 [32, 256, 512], P(('member', 'lat'), 'lon'), parts along dimension 0, may hold values 0 or 1
- ice_area: float32 [32, 256, 512], P(('member', 'lat'), 'lon'), parts along dimension 0, may hold values from 0.7 to 44.3
- route: int32 [32, 256], P(('member', 'lat'), 'lon'), parts along dimension 0, may hold values from 0 to 255, as said below
- ocean_area: float32 [2048, 2048], P(('member', 'lat'), 'lon'), parts along dimension 0, may hold values from 0.7 to 44.3
- ocean_wet: int32 [2048, 2048], P(('member', 'lat'), 'lon'), parts along dimension 0, may hold values 0 or 1
- exponent: int32 [8], replicated, may hold values from 0 to 3
Outputs:
- ocean_flux: float32 [8, 2048, 2048], P(None, ('member', 'lat'), 'lon'), parts along dimension 1
- source_total: float32 [32], P('member'), parts along dimension 0
The draws below stay inside these ranges and needn't reach their ends.
There are 4 independent parts, one for each index of `member`. The reference program is written for one: setup_inputs(seed, part) draws one part's arguments, and reference() takes and returns one part's arrays. A program takes and returns all parts, laid end to end along the dimension named above; an argument that names none is the same for every part. Nothing has to cross between parts.
Inputs may be any that keep to these rules, and one draw needn't show every extreme that they name: Within each latitude tile row, route is a permutation of 0 to 255. The 16 entries of one device name, for every longitude tile k that they name (route // 16 == k), exactly 2 blocks of it.
All inputs are finite; a program needn't handle non-finite values. No bound on the sum of `ice_mask` or of `ocean_wet` on one device may be relied on, other than what follows from the above.
Results may differ from the reference program's by a relative error of at most 0.0003.
Values sent between devices are 32-bit elements; how exact they have to be, the bound alone decides.
No kernel may reach another device: no remote copies, remote signals or barrier semaphores. Data moves between devices by JAX's collectives and lax.ppermute only.
A program may use at most 64 MiB of HBM per device.

```python
import jax
import jax.numpy as jnp

NF = 8
NBT = 16
BLAT = 4
CLON = 128
CLAT = 64
NLATG = 512
NLONG = 2048
N_LAT = 8
N_LON = 16


def shuffled(subkey):
    return jax.random.permutation(subkey, jnp.arange(NBT, dtype=jnp.int32))


def offsets_for(subkey):
    return jax.random.permutation(subkey, jnp.arange(N_LON, dtype=jnp.int32))[:NBT // max(2, NBT // N_LON)]


def make_route(key):
    capacity = max(2, NBT // N_LON)
    offset_count = NBT // capacity
    key_offsets, key_slots, key_positions = jax.random.split(jax.random.fold_in(key, 11), 3)
    offsets = jax.vmap(offsets_for)(jax.random.split(key_offsets, N_LAT))
    sequence = jax.vmap(shuffled)(jax.random.split(key_slots, N_LAT * N_LON)).reshape(N_LAT, N_LON, NBT)
    kind_index = sequence // capacity
    offset_table = jnp.broadcast_to(offsets[:, None, :], (N_LAT, N_LON, offset_count))
    chosen = jnp.take_along_axis(offset_table, kind_index, axis=2)
    source_tile = jnp.arange(N_LON, dtype=jnp.int32)[None, :, None]
    target_tile = (source_tile + chosen) % N_LON
    target_positions = jax.vmap(shuffled)(jax.random.split(key_positions, N_LAT * N_LON)).reshape(-1)
    row_number_index = jnp.arange(N_LAT, dtype=jnp.int32)[:, None, None]
    flat_index = (row_number_index * N_LON + target_tile) * NBT + sequence
    block_row = target_positions[flat_index]
    return (target_tile * NBT + block_row).reshape(N_LAT, N_LON * NBT).astype(jnp.int32)


def area_noise(key, shape):
    return jnp.exp(jax.random.uniform(key, shape, jnp.float32, jnp.log(0.7), jnp.log(1.4)))


def profile(lat_cell, lon_cell):
    return jnp.power(10.0, (lat_cell + 0.5) / NLATG) * jnp.power(10.0, 0.5 * (lon_cell + 0.5) / NLONG)


def draw_route(key, part):
    return make_route(key)


def draw_ice_area(key, part):
    route = make_route(key)
    target_tile = route // NBT
    block_row = route % NBT
    within = jnp.arange(BLAT * CLON, dtype=jnp.int32)
    lat_cell = jnp.arange(N_LAT, dtype=jnp.int32)[:, None, None] * CLAT + block_row[:, :, None] * BLAT + (within // CLON)[None, None, :]
    lon_cell = target_tile[:, :, None] * CLON + (within % CLON)[None, None, :]
    reshaped_grid = profile(lat_cell.astype(jnp.float32), lon_cell.astype(jnp.float32))
    return (reshaped_grid * area_noise(jax.random.fold_in(key, 23), reshaped_grid.shape)).astype(jnp.float32)


def draw_ocean_area(key, part):
    lat_cell = jnp.arange(NLATG, dtype=jnp.int32).astype(jnp.float32)[:, None]
    lon_cell = jnp.arange(NLONG, dtype=jnp.int32).astype(jnp.float32)[None, :]
    reshaped_grid = profile(lat_cell, lon_cell)
    return (reshaped_grid * area_noise(jax.random.fold_in(key, 31), reshaped_grid.shape)).astype(jnp.float32)


def touch_ends(entries, rng, low, top_value):
    longest = entries.shape.index(max(entries.shape))
    spots = []
    for shift in (0, 1):
        where = [jax.random.randint(jax.random.fold_in(rng, axis), (), 0, length) for axis, length in enumerate(entries.shape)]
        where[longest] = (where[longest] + shift) % entries.shape[longest]
        spots.append(tuple(where))
    return entries.at[spots[0]].set(low).at[spots[1]].set(top_value)


def steps_of(stream_key, shape, cuts, smallest, top_value):
    loudness, own = 1.0, jax.random.fold_in(stream_key, 6)
    for axis_at, parts in cuts:
        steps = jnp.exp(jax.random.uniform(jax.random.fold_in(own, axis_at), (parts,), jnp.float32, smallest / len(cuts), top_value / len(cuts)))
        loudness = loudness * jnp.repeat(steps, shape[axis_at] // parts).reshape([-1 if axis == axis_at else 1 for axis in range(len(shape))])
    return loudness


def setup_inputs(seed: int = 0, part: int = 0) -> dict:
    splits = jax.random.split(jax.random.key(seed), 9)
    own_keys = jax.random.split(jax.random.fold_in(splits[8], part), 9)
    ice_flux = jnp.clip(0.5 + 1.0 * jax.random.uniform(own_keys[0], (N_LAT, N_LON * NBT, NF, BLAT * CLON), jnp.float32) ** steps_of(own_keys[0], (N_LAT, N_LON * NBT, NF, BLAT * CLON), ((0, 8), (1, 16)), -0.2, 0.2), 0.5, 1.5)
    ice_frac = jnp.clip(0.05 + 0.95 * jax.random.uniform(own_keys[1], (N_LAT, N_LON * NBT, BLAT * CLON), jnp.float32) ** steps_of(own_keys[1], (N_LAT, N_LON * NBT, BLAT * CLON), ((0, 8), (1, 16)), -0.2, 0.2), 0.05, 1.0)
    ice_mask = touch_ends((jax.random.randint(own_keys[2], (N_LAT, N_LON * NBT, BLAT * CLON), 0, 4) < 3).astype(jnp.int32), jax.random.fold_in(own_keys[2], 1), 0, 1)
    ice_area = draw_ice_area(jax.random.fold_in(jax.random.fold_in(splits[8], part), 71), part)
    route = draw_route(jax.random.fold_in(jax.random.fold_in(splits[8], part), 71), part)
    ocean_area = draw_ocean_area(jax.random.fold_in(jax.random.fold_in(splits[8], part), 71), part)
    ocean_wet = touch_ends((jax.random.randint(own_keys[6], (NLATG, NLONG), 0, 4) < 3).astype(jnp.int32), jax.random.fold_in(own_keys[6], 1), 0, 1)
    exponent = touch_ends(jax.random.randint(splits[7], (NF,), 0, 4), jax.random.fold_in(splits[7], 1), 0, 3).astype(jnp.int32)
    return {"ice_flux": ice_flux, "ice_frac": ice_frac, "ice_mask": ice_mask, "ice_area": ice_area, "route": route, "ocean_area": ocean_area, "ocean_wet": ocean_wet, "exponent": exponent}


quantum = 1024.0
limb_base = 65536


def local_units(values, axes):
    return jnp.sum((values * quantum).astype(jnp.int32), axis=axes)


def split_units(total):
    upper_part = total // limb_base
    return upper_part, total - upper_part * limb_base


def join_units(upper_part, lower_part):
    return (upper_part.astype(jnp.float32) * limb_base + lower_part.astype(jnp.float32)) / quantum


def global_integral(units, axes):
    upper_part, lower_part = split_units(units)
    return join_units(jnp.sum(upper_part, axis=axes), jnp.sum(lower_part, axis=axes))


def reference(ice_flux, ice_frac, ice_mask, ice_area, route, ocean_area, ocean_wet, exponent):
    amount = ice_area * ice_frac * ice_mask.astype(jnp.float32)
    carried = ice_flux * amount[:, :, None, :]
    per_device = carried.reshape(N_LAT, N_LON, NBT, NF, BLAT * CLON)
    source = global_integral(local_units(per_device, (2, 4)), (0, 1))
    row_number_index = jnp.broadcast_to(jnp.arange(N_LAT, dtype=jnp.int32)[:, None], route.shape)
    block_groups = jnp.zeros_like(carried).at[row_number_index, route].set(carried)
    mapped = block_groups.reshape(N_LAT, N_LON, NBT, NF, BLAT, CLON).transpose(3, 0, 2, 4, 1, 5).reshape(NF, NLATG, NLONG)
    wet_cover = ocean_wet.astype(jnp.float32)
    wet_cell_terms = (wet_cover * mapped).reshape(NF, N_LAT, CLAT, N_LON, CLON)
    target = global_integral(local_units(wet_cell_terms, (2, 4)), (1, 2))
    area_terms = (ocean_area * wet_cover).reshape(N_LAT, CLAT, N_LON, CLON)
    wet_area = global_integral(local_units(area_terms, (1, 3)), (0, 1))
    correction = (source - target) / wet_area
    scaling = jnp.left_shift(jnp.ones_like(exponent), exponent).astype(jnp.float32)
    ocean_flux = wet_cover * scaling[:, None, None] * (mapped / ocean_area + correction[:, None, None])
    return ocean_flux, source * scaling
```

```python
import jax
import jax.numpy as jnp
from jax import lax
from jax.experimental import pallas as pl
from jax.experimental.pallas import tpu as pltpu
from jax.sharding import Mesh
from jax.sharding import PartitionSpec as P

MEMBER_LAT = ("member", "lat_0", "lat_1")

QUANTUM = 1024.0
LIMB_BITS = 16
LIMB_MASK = 65535
LANES = 128
VMEM_LIMIT = 16 * 1024 * 1024

TARGET_UPPER, TARGET_LOWER, SOURCE_UPPER, SOURCE_LOWER, WET_UPPER, WET_LOWER = 0, 8, 16, 24, 32, 33


def units(values):
    return (values * QUANTUM).astype(jnp.int32)


def spread(per_lane, first_upper, first_lower):
    upper = jnp.sum((per_lane >> LIMB_BITS).astype(jnp.float32), axis=1, keepdims=True)
    lower = jnp.sum((per_lane & LIMB_MASK).astype(jnp.float32), axis=1, keepdims=True)
    lane = lax.broadcasted_iota(jnp.int32, per_lane.shape, 1)
    row = lax.broadcasted_iota(jnp.int32, per_lane.shape, 0)
    placed = jnp.where(lane == row + first_upper, upper, 0.0) + jnp.where(lane == row + first_lower, lower, 0.0)
    return jnp.sum(placed, axis=0, keepdims=True).astype(jnp.int32)


def send_kernel(route, flux, frac, mask, area, ocean_area, ocean_wet, slots, rows, sums, taken):
    blocks = flux.shape[1]
    for i in range(rows.shape[0]):
        rows[i] = blocks
    for tile in range(rows.shape[0] // 2):
        taken[tile] = 0
    amount = area[0] * frac[0] * mask[0].astype(jnp.float32)
    total = jnp.zeros(flux.shape[2:], jnp.int32)
    for b in range(blocks):
        target = route[0, b]
        tile = target // blocks
        slot = 2 * tile + taken[tile]
        taken[tile] = taken[tile] + 1
        rows[slot] = target % blocks
        carried = flux[0, b] * amount[b : b + 1]
        slots[slot] = carried
        total = total + units(carried)
    per_lane = total[:, :LANES]
    for at in range(LANES, total.shape[1], LANES):
        per_lane = per_lane + total[:, at : at + LANES]
    wet = jnp.sum(units(ocean_area[...] * ocean_wet[...].astype(jnp.float32)), axis=0, keepdims=True)
    sums[...] = spread(per_lane, SOURCE_UPPER, SOURCE_LOWER) + spread(wet, WET_UPPER, WET_LOWER)


def place_kernel(lon, rows, received, sent_sums, exponent, ocean_area, ocean_wet, flux, sums, mapped):
    fields = received.shape[1]
    height, width = ocean_area.shape
    stride = mapped.shape[0] // fields
    band = received.shape[2] // width
    me = lon[0]
    for s in range(received.shape[0]):
        row = rows[s // 2, 2 * me + s % 2]
        for r in range(band):
            mapped[pl.ds(row * band + r, fields, stride), :] = received[s, :, r * width : (r + 1) * width]
    cover = ocean_wet[...].astype(jnp.float32)
    per_field = []
    for f in range(fields):
        field = mapped[f * stride : f * stride + height, :]
        per_field.append(jnp.sum(units(cover * field), axis=0, keepdims=True))
        scaling = jnp.left_shift(jnp.int32(1), exponent[f]).astype(jnp.float32)
        flux[f] = cover * scaling * (field / ocean_area[...])
    sums[...] = sent_sums[...] + spread(jnp.concatenate(per_field, axis=0), TARGET_UPPER, TARGET_LOWER)


def joined(sums, upper, lower):
    carry = jnp.right_shift(sums[0, lower], LIMB_BITS)
    high = (sums[0, upper] + carry).astype(jnp.float32)
    low = (sums[0, lower] - carry * (LIMB_MASK + 1)).astype(jnp.float32)
    return (high * float(LIMB_MASK + 1) + low) * (1.0 / QUANTUM)


def correct_kernel(sums, exponent, uncorrected, ocean_wet, flux, source_total):
    fields = uncorrected.shape[0]
    cover = ocean_wet[...].astype(jnp.float32)
    wet_area = jnp.full((1, LANES), joined(sums, WET_UPPER, WET_LOWER), jnp.float32)
    for f in range(fields):
        source = joined(sums, SOURCE_UPPER + f, SOURCE_LOWER + f)
        target = joined(sums, TARGET_UPPER + f, TARGET_LOWER + f)
        scaling = jnp.left_shift(jnp.int32(1), exponent[f]).astype(jnp.float32)
        correction = jnp.full((1, LANES), source - target, jnp.float32) / wet_area
        flux[f] = uncorrected[f] + cover * (correction * scaling)
        source_total[f] = source * scaling


def body(ice_flux, ice_frac, ice_mask, ice_area, route, ocean_area, ocean_wet, exponent):
    blocks, fields, cells = ice_flux.shape[1:]
    height, width = ocean_area.shape
    tiles = lax.axis_size("lon")
    vmem = pl.BlockSpec(memory_space=pltpu.VMEM)
    smem = pl.BlockSpec(memory_space=pltpu.SMEM)
    params = pltpu.CompilerParams(vmem_limit_bytes=VMEM_LIMIT)
    slots, rows, sums = pl.pallas_call(
        send_kernel,
        out_shape=(
            jax.ShapeDtypeStruct((2 * tiles, fields, cells), jnp.float32),
            jax.ShapeDtypeStruct((2 * tiles,), jnp.int32),
            jax.ShapeDtypeStruct((1, LANES), jnp.int32),
        ),
        in_specs=[smem] + [vmem] * 6,
        out_specs=(vmem, smem, vmem),
        scratch_shapes=[pltpu.SMEM((tiles,), jnp.int32)],
        compiler_params=params,
    )(route, ice_flux, ice_frac, ice_mask, ice_area, ocean_area, ocean_wet)
    received = lax.all_to_all(slots, "lon", 0, 0, tiled=True)
    all_rows = lax.all_gather(rows, "lon")
    lon = lax.axis_index("lon").astype(jnp.int32).reshape(1)
    uncorrected, sums = pl.pallas_call(
        place_kernel,
        out_shape=(
            jax.ShapeDtypeStruct((fields, height, width), jnp.float32),
            jax.ShapeDtypeStruct((1, LANES), jnp.int32),
        ),
        in_specs=[smem, smem, vmem, vmem, smem, vmem, vmem],
        out_specs=(vmem, vmem),
        scratch_shapes=[pltpu.VMEM((fields * (height + 8), width), jnp.float32)],
        compiler_params=params,
    )(lon, all_rows, received, sums, exponent, ocean_area, ocean_wet)
    sums = lax.psum(lax.psum(sums, ("lat_0", "lat_1")), "lon")
    return pl.pallas_call(
        correct_kernel,
        out_shape=(
            jax.ShapeDtypeStruct((fields, height, width), jnp.float32),
            jax.ShapeDtypeStruct((fields,), jnp.float32),
        ),
        in_specs=[smem, smem, vmem, vmem],
        out_specs=(vmem, smem),
        compiler_params=params,
    )(sums, exponent, uncorrected, ocean_wet)


def solution(mesh):
    torus = Mesh(
        mesh.devices.reshape(mesh.shape["member"], 4, 2, mesh.shape["lon"]),
        ("member", "lat_0", "lat_1", "lon"),
    )
    in_specs = (
        P(MEMBER_LAT, "lon", None, None),
        P(MEMBER_LAT, "lon", None),
        P(MEMBER_LAT, "lon", None),
        P(MEMBER_LAT, "lon", None),
        P(MEMBER_LAT, "lon"),
        P(MEMBER_LAT, "lon"),
        P(MEMBER_LAT, "lon"),
        P(),
    )
    out_specs = (P(None, MEMBER_LAT, "lon"), P("member"))
    return jax.shard_map(body, mesh=torus, in_specs=in_specs, out_specs=out_specs, check_vma=False)
```

```python
import jax
import jax.numpy as jnp
from jax import lax
from jax.experimental import pallas as pl
from jax.experimental.pallas import tpu as pltpu
from jax.sharding import Mesh
from jax.sharding import PartitionSpec as P

MEMBER_LAT = ("member", "lat_0", "lat_1")
LAT = ("lat_0", "lat_1")

QUANTUM = 1024.0
LIMB_BITS = 16
LIMB_MASK = 65535
LANES = 128
VMEM_LIMIT = 16 * 1024 * 1024
SEND_VMEM_LIMIT = 62 * 1024 * 1024
PIECES = 4

TARGET, SOURCE, WET = 0, 16, 32
LOWER = 8


def units(values):
    return (values * QUANTUM).astype(jnp.int32)


def spread(per_lane, first):
    upper = jnp.sum((per_lane >> LIMB_BITS).astype(jnp.float32), axis=1, keepdims=True)
    lower = jnp.sum((per_lane & LIMB_MASK).astype(jnp.float32), axis=1, keepdims=True)
    lane = lax.broadcasted_iota(jnp.int32, per_lane.shape, 1)
    row = lax.broadcasted_iota(jnp.int32, per_lane.shape, 0)
    placed = jnp.where(lane == row + first, upper, 0.0) + jnp.where(lane == row + first + LOWER, lower, 0.0)
    return jnp.sum(placed, axis=0, keepdims=True).astype(jnp.int32)


def send_kernel(route, flux, frac, mask, area, chunks, route_s, flux_v, frac_v, mask_v, area_v, taken, sems):
    blocks, fields, cells = flux_v.shape
    tiles = chunks.shape[0]
    band = cells // LANES
    copies = [
        pltpu.make_async_copy(route.at[0], route_s, sems.at[0]),
        pltpu.make_async_copy(frac.at[0], frac_v, sems.at[1]),
        pltpu.make_async_copy(mask.at[0], mask_v, sems.at[2]),
        pltpu.make_async_copy(area.at[0], area_v, sems.at[3]),
    ]
    piece = blocks // PIECES
    for p in range(PIECES):
        part = pl.ds(p * piece, piece)
        copies.append(pltpu.make_async_copy(flux.at[0, part], flux_v.at[part], sems.at[4 + p]))
    for copy in copies:
        copy.start()
    for tile in range(tiles):
        taken[tile] = 0
    nobody = jnp.full((8, LANES), float(blocks), jnp.float32)
    for tile in range(tiles):
        chunks[tile, 2 * band * fields :, :] = nobody
    for copy in copies[:4]:
        copy.wait()
    amount = area_v[...] * frac_v[...] * mask_v[...].astype(jnp.float32)
    for b in range(blocks):
        if b % piece == 0:
            copies[4 + b // piece].wait()
        target = route_s[b]
        tile = target // blocks
        order = taken[tile]
        taken[tile] = order + 1
        carried = flux_v[b] * amount[b : b + 1]
        first = pl.multiple_of(order * (band * fields), band * fields)
        for r in range(band):
            chunks[tile, pl.ds(first + r * fields, fields), :] = carried[:, r * LANES : (r + 1) * LANES]
        row = jnp.full((1, LANES), target % blocks, jnp.int32).astype(jnp.float32)
        chunks[tile, pl.ds(2 * band * fields + order, 1), :] = row


def beside_kernel(exponent, flux, frac, mask, area, ocean_area, ocean_wet, sums, scaling):
    amount = area[0] * frac[0] * mask[0].astype(jnp.float32)
    total = jnp.zeros(flux.shape[2:], jnp.int32)
    for b in range(flux.shape[1]):
        total = total + units(flux[0, b] * amount[b : b + 1])
    per_lane = total[:, :LANES]
    for at in range(LANES, total.shape[1], LANES):
        per_lane = per_lane + total[:, at : at + LANES]
    wet = jnp.sum(units(ocean_area[...] * ocean_wet[...].astype(jnp.float32)), axis=0, keepdims=True)
    sums[...] = spread(per_lane, SOURCE) + spread(wet, WET)
    lane = lax.broadcasted_iota(jnp.int32, (1, LANES), 1)
    scales = jnp.ones((1, LANES), jnp.int32)
    for f in range(flux.shape[2]):
        scales = jnp.where(lane == f, jnp.left_shift(jnp.int32(1), exponent[f]), scales)
    scaling[...] = scales.astype(jnp.float32)


def place_kernel(received, sent_sums, ocean_area, ocean_wet, quotient, sums, mapped):
    fields, height, width = quotient.shape
    stride = mapped.shape[0] // fields
    band = (received.shape[1] - 8) // (2 * fields)
    for s in range(received.shape[0]):
        for order in range(2):
            at = (2 * s + order) * band * fields
            row = received[s, 2 * band * fields + order, 0].astype(jnp.int32)
            for r in range(band):
                first = (order * band + r) * fields
                mapped[pl.ds(row * band + r, fields, stride), :] = received[s, first : first + fields, :]
    cover = ocean_wet[...].astype(jnp.float32)
    per_field = []
    for f in range(fields):
        field = mapped[f * stride : f * stride + height, :]
        per_field.append(jnp.sum(units(cover * field), axis=0, keepdims=True))
        quotient[f] = field / ocean_area[...]
    sums[...] = sent_sums[...] + spread(jnp.concatenate(per_field, axis=0), TARGET)


def correct_kernel(sums, scaling, quotient, ocean_wet, flux, source_total):
    fields = quotient.shape[0]
    upper = jnp.broadcast_to(sums[...], (8, LANES))
    lower = pltpu.roll(upper, LANES - LOWER, 1)
    upper = (upper + (lower >> LIMB_BITS)).astype(jnp.float32)
    integral = (upper * float(LIMB_MASK + 1) + (lower & LIMB_MASK).astype(jnp.float32)) * (1.0 / QUANTUM)
    source = pltpu.roll(integral, LANES - (SOURCE - TARGET), 1)
    lane = lax.broadcasted_iota(jnp.int32, (8, LANES), 1)
    row = lax.broadcasted_iota(jnp.int32, (8, LANES), 0)
    wet_area = jnp.sum(jnp.where(lane == WET, integral, 0.0), axis=1, keepdims=True)
    correction = (source - integral) / wet_area
    scales = jnp.broadcast_to(scaling[...], (8, LANES))
    per_field = jnp.sum(jnp.where(lane == row, correction, 0.0), axis=1, keepdims=True)
    scale = jnp.sum(jnp.where(lane == row, scales, 0.0), axis=1, keepdims=True)
    cover = ocean_wet[...].astype(jnp.float32)
    for f in range(fields):
        flux[f] = cover * scale[f : f + 1] * (quotient[f] + per_field[f : f + 1])
    source_total[...] = (source * scales)[0, :fields]


def body(ice_flux, ice_frac, ice_mask, ice_area, route, ocean_area, ocean_wet, exponent):
    blocks, fields, cells = ice_flux.shape[1:]
    height, width = ocean_area.shape
    tiles = lax.axis_size("lon")
    chunk_rows = 2 * fields * cells // LANES + 8
    vmem = pl.BlockSpec(memory_space=pltpu.VMEM)
    smem = pl.BlockSpec(memory_space=pltpu.SMEM)
    hbm = pl.BlockSpec(memory_space=pltpu.HBM)
    params = pltpu.CompilerParams(vmem_limit_bytes=VMEM_LIMIT)
    chunks = pl.pallas_call(
        send_kernel,
        out_shape=jax.ShapeDtypeStruct((tiles, chunk_rows, LANES), jnp.float32),
        in_specs=[hbm] * 5,
        out_specs=vmem,
        scratch_shapes=[
            pltpu.SMEM((blocks,), jnp.int32),
            pltpu.VMEM((blocks, fields, cells), jnp.float32),
            pltpu.VMEM((blocks, cells), jnp.float32),
            pltpu.VMEM((blocks, cells), jnp.int32),
            pltpu.VMEM((blocks, cells), jnp.float32),
            pltpu.SMEM((tiles,), jnp.int32),
            pltpu.SemaphoreType.DMA((4 + PIECES,)),
        ],
        compiler_params=pltpu.CompilerParams(vmem_limit_bytes=SEND_VMEM_LIMIT),
    )(route, ice_flux, ice_frac, ice_mask, ice_area)
    received = lax.all_to_all(chunks, "lon", 0, 0, tiled=True)
    sums, scaling = pl.pallas_call(
        beside_kernel,
        out_shape=(
            jax.ShapeDtypeStruct((1, LANES), jnp.int32),
            jax.ShapeDtypeStruct((1, LANES), jnp.float32),
        ),
        in_specs=[smem] + [vmem] * 6,
        out_specs=(vmem, vmem),
        compiler_params=params,
    )(exponent, ice_flux, ice_frac, ice_mask, ice_area, ocean_area, ocean_wet)
    quotient, sums = pl.pallas_call(
        place_kernel,
        out_shape=(
            jax.ShapeDtypeStruct((fields, height, width), jnp.float32),
            jax.ShapeDtypeStruct((1, LANES), jnp.int32),
        ),
        in_specs=[vmem] * 4,
        out_specs=(vmem, vmem),
        scratch_shapes=[pltpu.VMEM((fields * (height + 8), width), jnp.float32)],
        compiler_params=params,
    )(received, sums, ocean_area, ocean_wet)
    sums = lax.psum(lax.psum(sums, LAT), "lon")
    return pl.pallas_call(
        correct_kernel,
        out_shape=(
            jax.ShapeDtypeStruct((fields, height, width), jnp.float32),
            jax.ShapeDtypeStruct((fields,), jnp.float32),
        ),
        in_specs=[vmem] * 4,
        out_specs=(vmem, vmem),
        compiler_params=params,
    )(sums, scaling, quotient, ocean_wet)


def solution(mesh):
    torus = Mesh(
        mesh.devices.reshape(mesh.shape["member"], 4, 2, mesh.shape["lon"]),
        ("member", "lat_0", "lat_1", "lon"),
    )
    in_specs = (
        P(MEMBER_LAT, "lon", None, None),
        P(MEMBER_LAT, "lon", None),
        P(MEMBER_LAT, "lon", None),
        P(MEMBER_LAT, "lon", None),
        P(MEMBER_LAT, "lon"),
        P(MEMBER_LAT, "lon"),
        P(MEMBER_LAT, "lon"),
        P(),
    )
    out_specs = (P(None, MEMBER_LAT, "lon"), P("member"))
    return jax.shard_map(body, mesh=torus, in_specs=in_specs, out_specs=out_specs, check_vma=False)
```

```python
import jax
import jax.numpy as jnp
from jax import lax
from jax.experimental import pallas as pl
from jax.experimental.pallas import tpu as pltpu
from jax.sharding import Mesh
from jax.sharding import PartitionSpec as P

MEMBER_LAT = ("member", "lat_0", "lat_1")
LAT = ("lat_0", "lat_1")

QUANTUM = 1024.0
LIMB_BITS = 16
LIMB_MASK = 65535
LANES = 128
VMEM_LIMIT = 16 * 1024 * 1024
SEND_VMEM_LIMIT = 62 * 1024 * 1024
PIECES = 4

TARGET, SOURCE, WET = 0, 16, 32
LOWER = 8


def units(values):
    return (values * QUANTUM).astype(jnp.int32)


def spread(per_lane, first):
    upper = jnp.sum((per_lane >> LIMB_BITS).astype(jnp.float32), axis=1, keepdims=True)
    lower = jnp.sum((per_lane & LIMB_MASK).astype(jnp.float32), axis=1, keepdims=True)
    lane = lax.broadcasted_iota(jnp.int32, per_lane.shape, 1)
    row = lax.broadcasted_iota(jnp.int32, per_lane.shape, 0)
    placed = jnp.where(lane == row + first, upper, 0.0) + jnp.where(lane == row + first + LOWER, lower, 0.0)
    return jnp.sum(placed, axis=0, keepdims=True).astype(jnp.int32)


def send_kernel(route, flux, frac, mask, area, chunks, route_s, flux_v, frac_v, mask_v, area_v, staged, rows, taken, place, in_sems, out_sems):
    blocks, fields, cells = flux_v.shape
    tiles = chunks.shape[0]
    band = cells // LANES
    block_rows = band * fields
    route_in = pltpu.make_async_copy(route.at[0], route_s, in_sems.at[0])
    frac_in = pltpu.make_async_copy(frac.at[0], frac_v, in_sems.at[1])
    mask_in = pltpu.make_async_copy(mask.at[0], mask_v, in_sems.at[2])
    area_in = pltpu.make_async_copy(area.at[0], area_v, in_sems.at[3])
    piece = blocks // PIECES
    flux_in = []
    for p in range(PIECES):
        part = pl.ds(p * piece, piece)
        flux_in.append(pltpu.make_async_copy(flux.at[0, part], flux_v.at[part], in_sems.at[4 + p]))
    for copy in [route_in, frac_in, mask_in, area_in] + flux_in:
        copy.start()
    for tile in range(tiles):
        taken[tile] = 0
    nobody = jnp.full((8, LANES), float(blocks), jnp.float32)
    for tile in range(tiles):
        rows[tile] = nobody
    route_in.wait()
    for b in range(blocks):
        target = route_s[b]
        tile = target // blocks
        order = taken[tile]
        taken[tile] = order + 1
        place[b] = 2 * tile + order
        rows[tile, pl.ds(order, 1), :] = jnp.full((1, LANES), target % blocks, jnp.int32).astype(jnp.float32)
    rows_out = pltpu.make_async_copy(rows, chunks.at[:, pl.ds(2 * block_rows, 8)], out_sems.at[blocks])
    rows_out.start()
    frac_in.wait()
    mask_in.wait()
    area_in.wait()
    amount = area_v[...] * frac_v[...] * mask_v[...].astype(jnp.float32)
    blocks_out = []
    for b in range(blocks):
        if b % piece == 0:
            flux_in[b // piece].wait()
        carried = flux_v[b] * amount[b : b + 1]
        for r in range(band):
            staged[b, r * fields : (r + 1) * fields, :] = carried[:, r * LANES : (r + 1) * LANES]
        first = pl.multiple_of((place[b] % 2) * block_rows, block_rows)
        to = chunks.at[place[b] // 2, pl.ds(first, block_rows)]
        blocks_out.append(pltpu.make_async_copy(staged.at[b], to, out_sems.at[b]))
        blocks_out[b].start()
    rows_out.wait()
    for copy in blocks_out:
        copy.wait()


def beside_kernel(exponent, flux, frac, mask, area, ocean_area, ocean_wet, sums, scaling):
    amount = area[0] * frac[0] * mask[0].astype(jnp.float32)
    total = jnp.zeros(flux.shape[2:], jnp.int32)
    for b in range(flux.shape[1]):
        total = total + units(flux[0, b] * amount[b : b + 1])
    per_lane = total[:, :LANES]
    for at in range(LANES, total.shape[1], LANES):
        per_lane = per_lane + total[:, at : at + LANES]
    wet = jnp.sum(units(ocean_area[...] * ocean_wet[...].astype(jnp.float32)), axis=0, keepdims=True)
    sums[...] = spread(per_lane, SOURCE) + spread(wet, WET)
    lane = lax.broadcasted_iota(jnp.int32, (1, LANES), 1)
    scales = jnp.ones((1, LANES), jnp.int32)
    for f in range(flux.shape[2]):
        scales = jnp.where(lane == f, jnp.left_shift(jnp.int32(1), exponent[f]), scales)
    scaling[...] = scales.astype(jnp.float32)


def place_kernel(received, sent_sums, ocean_area, ocean_wet, quotient, sums, mapped):
    fields, height, width = quotient.shape
    stride = mapped.shape[0] // fields
    band = (received.shape[1] - 8) // (2 * fields)
    for s in range(received.shape[0]):
        for order in range(2):
            at = (2 * s + order) * band * fields
            row = received[s, 2 * band * fields + order, 0].astype(jnp.int32)
            for r in range(band):
                first = (order * band + r) * fields
                mapped[pl.ds(row * band + r, fields, stride), :] = received[s, first : first + fields, :]
    cover = ocean_wet[...].astype(jnp.float32)
    per_field = []
    for f in range(fields):
        field = mapped[f * stride : f * stride + height, :]
        per_field.append(jnp.sum(units(cover * field), axis=0, keepdims=True))
        quotient[f] = field / ocean_area[...]
    sums[...] = sent_sums[...] + spread(jnp.concatenate(per_field, axis=0), TARGET)


def correct_kernel(sums, scaling, quotient, ocean_wet, flux, source_total):
    fields = quotient.shape[0]
    upper = jnp.broadcast_to(sums[...], (8, LANES))
    lower = pltpu.roll(upper, LANES - LOWER, 1)
    upper = (upper + (lower >> LIMB_BITS)).astype(jnp.float32)
    integral = (upper * float(LIMB_MASK + 1) + (lower & LIMB_MASK).astype(jnp.float32)) * (1.0 / QUANTUM)
    source = pltpu.roll(integral, LANES - (SOURCE - TARGET), 1)
    lane = lax.broadcasted_iota(jnp.int32, (8, LANES), 1)
    row = lax.broadcasted_iota(jnp.int32, (8, LANES), 0)
    wet_area = jnp.sum(jnp.where(lane == WET, integral, 0.0), axis=1, keepdims=True)
    correction = (source - integral) / wet_area
    scales = jnp.broadcast_to(scaling[...], (8, LANES))
    per_field = jnp.sum(jnp.where(lane == row, correction, 0.0), axis=1, keepdims=True)
    scale = jnp.sum(jnp.where(lane == row, scales, 0.0), axis=1, keepdims=True)
    cover = ocean_wet[...].astype(jnp.float32)
    for f in range(fields):
        flux[f] = cover * scale[f : f + 1] * (quotient[f] + per_field[f : f + 1])
    source_total[...] = (source * scales)[0, :fields]


def body(ice_flux, ice_frac, ice_mask, ice_area, route, ocean_area, ocean_wet, exponent):
    blocks, fields, cells = ice_flux.shape[1:]
    height, width = ocean_area.shape
    tiles = lax.axis_size("lon")
    chunk_rows = 2 * fields * cells // LANES + 8
    vmem = pl.BlockSpec(memory_space=pltpu.VMEM)
    smem = pl.BlockSpec(memory_space=pltpu.SMEM)
    hbm = pl.BlockSpec(memory_space=pltpu.HBM)
    params = pltpu.CompilerParams(vmem_limit_bytes=VMEM_LIMIT)
    chunks = pl.pallas_call(
        send_kernel,
        out_shape=jax.ShapeDtypeStruct((tiles, chunk_rows, LANES), jnp.float32),
        in_specs=[hbm] * 5,
        out_specs=hbm,
        scratch_shapes=[
            pltpu.SMEM((blocks,), jnp.int32),
            pltpu.VMEM((blocks, fields, cells), jnp.float32),
            pltpu.VMEM((blocks, cells), jnp.float32),
            pltpu.VMEM((blocks, cells), jnp.int32),
            pltpu.VMEM((blocks, cells), jnp.float32),
            pltpu.VMEM((blocks, fields * cells // LANES, LANES), jnp.float32),
            pltpu.VMEM((tiles, 8, LANES), jnp.float32),
            pltpu.SMEM((tiles,), jnp.int32),
            pltpu.SMEM((blocks,), jnp.int32),
            pltpu.SemaphoreType.DMA((4 + PIECES,)),
            pltpu.SemaphoreType.DMA((blocks + 1,)),
        ],
        compiler_params=pltpu.CompilerParams(vmem_limit_bytes=SEND_VMEM_LIMIT),
    )(route, ice_flux, ice_frac, ice_mask, ice_area)
    received = lax.all_to_all(chunks, "lon", 0, 0, tiled=True)
    sums, scaling = pl.pallas_call(
        beside_kernel,
        out_shape=(
            jax.ShapeDtypeStruct((1, LANES), jnp.int32),
            jax.ShapeDtypeStruct((1, LANES), jnp.float32),
        ),
        in_specs=[smem] + [vmem] * 6,
        out_specs=(vmem, vmem),
        compiler_params=params,
    )(exponent, ice_flux, ice_frac, ice_mask, ice_area, ocean_area, ocean_wet)
    quotient, sums = pl.pallas_call(
        place_kernel,
        out_shape=(
            jax.ShapeDtypeStruct((fields, height, width), jnp.float32),
            jax.ShapeDtypeStruct((1, LANES), jnp.int32),
        ),
        in_specs=[vmem] * 4,
        out_specs=(vmem, vmem),
        scratch_shapes=[pltpu.VMEM((fields * (height + 8), width), jnp.float32)],
        compiler_params=params,
    )(received, sums, ocean_area, ocean_wet)
    sums = lax.psum(sums, LAT + ("lon",))
    return pl.pallas_call(
        correct_kernel,
        out_shape=(
            jax.ShapeDtypeStruct((fields, height, width), jnp.float32),
            jax.ShapeDtypeStruct((fields,), jnp.float32),
        ),
        in_specs=[vmem] * 4,
        out_specs=(vmem, vmem),
        compiler_params=params,
    )(sums, scaling, quotient, ocean_wet)


def solution(mesh):
    torus = Mesh(
        mesh.devices.reshape(mesh.shape["member"], 4, 2, mesh.shape["lon"]),
        ("member", "lat_0", "lat_1", "lon"),
    )
    in_specs = (
        P(MEMBER_LAT, "lon", None, None),
        P(MEMBER_LAT, "lon", None),
        P(MEMBER_LAT, "lon", None),
        P(MEMBER_LAT, "lon", None),
        P(MEMBER_LAT, "lon"),
        P(MEMBER_LAT, "lon"),
        P(MEMBER_LAT, "lon"),
        P(),
    )
    out_specs = (P(None, MEMBER_LAT, "lon"), P("member"))
    return jax.shard_map(body, mesh=torus, in_specs=in_specs, out_specs=out_specs, check_vma=False)
```

```python
import jax
import jax.numpy as jnp
from jax import lax
from jax.experimental import pallas as pl
from jax.experimental.pallas import tpu as pltpu
from jax.sharding import Mesh
from jax.sharding import PartitionSpec as P

MEMBER_LAT = ("member", "lat_0", "lat_1")
LAT = ("lat_0", "lat_1")

QUANTUM = 1024.0
LIMB_BITS = 16
LIMB_MASK = 65535
LANES = 128
VMEM_LIMIT = 16 * 1024 * 1024
SEND_VMEM_LIMIT = 62 * 1024 * 1024
PIECES = 4

TARGET, SOURCE, WET = 0, 16, 32
LOWER = 8


def units(values):
    return (values * QUANTUM).astype(jnp.int32)


def spread(per_lane, first):
    upper = jnp.sum((per_lane >> LIMB_BITS).astype(jnp.float32), axis=1, keepdims=True)
    lower = jnp.sum((per_lane & LIMB_MASK).astype(jnp.float32), axis=1, keepdims=True)
    lane = lax.broadcasted_iota(jnp.int32, per_lane.shape, 1)
    row = lax.broadcasted_iota(jnp.int32, per_lane.shape, 0)
    placed = jnp.where(lane == row + first, upper, 0.0) + jnp.where(lane == row + first + LOWER, lower, 0.0)
    return jnp.sum(placed, axis=0, keepdims=True).astype(jnp.int32)


def send_kernel(route, flux, frac, mask, area, chunks, route_s, flux_v, frac_v, mask_v, area_v, staged, rows, taken, place, in_sems, out_sems):
    blocks, fields, cells = flux_v.shape
    tiles = chunks.shape[0]
    band = cells // LANES
    block_rows = band * fields
    route_in = pltpu.make_async_copy(route.at[0], route_s, in_sems.at[0])
    frac_in = pltpu.make_async_copy(frac.at[0], frac_v, in_sems.at[1])
    mask_in = pltpu.make_async_copy(mask.at[0], mask_v, in_sems.at[2])
    area_in = pltpu.make_async_copy(area.at[0], area_v, in_sems.at[3])
    piece = blocks // PIECES
    flux_in = []
    for p in range(PIECES):
        part = pl.ds(p * piece, piece)
        flux_in.append(pltpu.make_async_copy(flux.at[0, part], flux_v.at[part], in_sems.at[4 + p]))
    for copy in [route_in, frac_in, mask_in, area_in] + flux_in:
        copy.start()
    for tile in range(tiles):
        taken[tile] = 0
    nobody = jnp.full((8, LANES), float(blocks), jnp.float32)
    for tile in range(tiles):
        rows[tile] = nobody
    route_in.wait()
    for b in range(blocks):
        target = route_s[b]
        tile = target // blocks
        order = taken[tile]
        taken[tile] = order + 1
        at = (tile + (tiles - tiles // 2)) % tiles
        place[b] = 2 * at + order
        rows[at, pl.ds(order, 1), :] = jnp.full((1, LANES), target % blocks, jnp.int32).astype(jnp.float32)
    rows_out = pltpu.make_async_copy(rows, chunks.at[:, pl.ds(2 * block_rows, 8)], out_sems.at[blocks])
    rows_out.start()
    frac_in.wait()
    mask_in.wait()
    area_in.wait()
    amount = area_v[...] * frac_v[...] * mask_v[...].astype(jnp.float32)
    blocks_out = []
    for b in range(blocks):
        if b % piece == 0:
            flux_in[b // piece].wait()
        carried = flux_v[b] * amount[b : b + 1]
        for r in range(band):
            staged[b, r * fields : (r + 1) * fields, :] = carried[:, r * LANES : (r + 1) * LANES]
        first = pl.multiple_of((place[b] % 2) * block_rows, block_rows)
        to = chunks.at[place[b] // 2, pl.ds(first, block_rows)]
        blocks_out.append(pltpu.make_async_copy(staged.at[b], to, out_sems.at[b]))
        blocks_out[b].start()
    rows_out.wait()
    for copy in blocks_out:
        copy.wait()


def beside_kernel(exponent, flux, frac, mask, area, ocean_area, ocean_wet, sums, scaling):
    amount = area[0] * frac[0] * mask[0].astype(jnp.float32)
    total = jnp.zeros(flux.shape[2:], jnp.int32)
    for b in range(flux.shape[1]):
        total = total + units(flux[0, b] * amount[b : b + 1])
    per_lane = total[:, :LANES]
    for at in range(LANES, total.shape[1], LANES):
        per_lane = per_lane + total[:, at : at + LANES]
    wet = jnp.sum(units(ocean_area[...] * ocean_wet[...].astype(jnp.float32)), axis=0, keepdims=True)
    sums[...] = spread(per_lane, SOURCE) + spread(wet, WET)
    lane = lax.broadcasted_iota(jnp.int32, (1, LANES), 1)
    scales = jnp.ones((1, LANES), jnp.int32)
    for f in range(flux.shape[2]):
        scales = jnp.where(lane == f, jnp.left_shift(jnp.int32(1), exponent[f]), scales)
    scaling[...] = scales.astype(jnp.float32)


def place_kernel(received, sent_sums, ocean_area, ocean_wet, quotient, sums, mapped):
    fields, height, width = quotient.shape
    stride = mapped.shape[0] // fields
    band = (received.shape[1] - 8) // (2 * fields)
    for s in range(received.shape[0]):
        for order in range(2):
            at = (2 * s + order) * band * fields
            row = received[s, 2 * band * fields + order, 0].astype(jnp.int32)
            for r in range(band):
                first = (order * band + r) * fields
                mapped[pl.ds(row * band + r, fields, stride), :] = received[s, first : first + fields, :]
    cover = ocean_wet[...].astype(jnp.float32)
    per_field = []
    for f in range(fields):
        field = mapped[f * stride : f * stride + height, :]
        per_field.append(jnp.sum(units(cover * field), axis=0, keepdims=True))
        quotient[f] = field / ocean_area[...]
    own = sent_sums[...] + spread(jnp.concatenate(per_field, axis=0), TARGET)
    for tile in range(sums.shape[0]):
        sums[tile] = own


def correct_kernel(sums, scaling, quotient, ocean_wet, flux, source_total):
    fields = quotient.shape[0]
    whole = sums[0]
    for tile in range(1, sums.shape[0]):
        whole = whole + sums[tile]
    upper = jnp.broadcast_to(whole, (8, LANES))
    lower = pltpu.roll(upper, LANES - LOWER, 1)
    upper = (upper + (lower >> LIMB_BITS)).astype(jnp.float32)
    integral = (upper * float(LIMB_MASK + 1) + (lower & LIMB_MASK).astype(jnp.float32)) * (1.0 / QUANTUM)
    source = pltpu.roll(integral, LANES - (SOURCE - TARGET), 1)
    lane = lax.broadcasted_iota(jnp.int32, (8, LANES), 1)
    row = lax.broadcasted_iota(jnp.int32, (8, LANES), 0)
    wet_area = jnp.sum(jnp.where(lane == WET, integral, 0.0), axis=1, keepdims=True)
    correction = (source - integral) / wet_area
    scales = jnp.broadcast_to(scaling[...], (8, LANES))
    per_field = jnp.sum(jnp.where(lane == row, correction, 0.0), axis=1, keepdims=True)
    scale = jnp.sum(jnp.where(lane == row, scales, 0.0), axis=1, keepdims=True)
    cover = ocean_wet[...].astype(jnp.float32)
    for f in range(fields):
        flux[f] = cover * scale[f : f + 1] * (quotient[f] + per_field[f : f + 1])
    source_total[...] = (source * scales)[0, :fields]


def exchange(chunks):
    tiles = lax.axis_size("lon")
    order = [(tiles // 2 + i) % tiles for i in range(tiles)]
    return lax.all_to_all(chunks, "lon", 0, 0, axis_index_groups=[order], tiled=True)


def body(ice_flux, ice_frac, ice_mask, ice_area, route, ocean_area, ocean_wet, exponent):
    blocks, fields, cells = ice_flux.shape[1:]
    height, width = ocean_area.shape
    tiles = lax.axis_size("lon")
    chunk_rows = 2 * fields * cells // LANES + 8
    vmem = pl.BlockSpec(memory_space=pltpu.VMEM)
    smem = pl.BlockSpec(memory_space=pltpu.SMEM)
    hbm = pl.BlockSpec(memory_space=pltpu.HBM)
    params = pltpu.CompilerParams(vmem_limit_bytes=VMEM_LIMIT)
    chunks = pl.pallas_call(
        send_kernel,
        out_shape=jax.ShapeDtypeStruct((tiles, chunk_rows, LANES), jnp.float32),
        in_specs=[hbm] * 5,
        out_specs=hbm,
        scratch_shapes=[
            pltpu.SMEM((blocks,), jnp.int32),
            pltpu.VMEM((blocks, fields, cells), jnp.float32),
            pltpu.VMEM((blocks, cells), jnp.float32),
            pltpu.VMEM((blocks, cells), jnp.int32),
            pltpu.VMEM((blocks, cells), jnp.float32),
            pltpu.VMEM((blocks, fields * cells // LANES, LANES), jnp.float32),
            pltpu.VMEM((tiles, 8, LANES), jnp.float32),
            pltpu.SMEM((tiles,), jnp.int32),
            pltpu.SMEM((blocks,), jnp.int32),
            pltpu.SemaphoreType.DMA((4 + PIECES,)),
            pltpu.SemaphoreType.DMA((blocks + 1,)),
        ],
        compiler_params=pltpu.CompilerParams(vmem_limit_bytes=SEND_VMEM_LIMIT),
    )(route, ice_flux, ice_frac, ice_mask, ice_area)
    received = exchange(chunks)
    sums, scaling = pl.pallas_call(
        beside_kernel,
        out_shape=(
            jax.ShapeDtypeStruct((1, LANES), jnp.int32),
            jax.ShapeDtypeStruct((1, LANES), jnp.float32),
        ),
        in_specs=[smem] + [vmem] * 6,
        out_specs=(vmem, vmem),
        compiler_params=params,
    )(exponent, ice_flux, ice_frac, ice_mask, ice_area, ocean_area, ocean_wet)
    quotient, sums = pl.pallas_call(
        place_kernel,
        out_shape=(
            jax.ShapeDtypeStruct((fields, height, width), jnp.float32),
            jax.ShapeDtypeStruct((tiles, 1, LANES), jnp.int32),
        ),
        in_specs=[vmem] * 4,
        out_specs=(vmem, vmem),
        scratch_shapes=[pltpu.VMEM((fields * (height + 8), width), jnp.float32)],
        compiler_params=params,
    )(received, sums, ocean_area, ocean_wet)
    sums = exchange(lax.psum(sums, LAT))
    return pl.pallas_call(
        correct_kernel,
        out_shape=(
            jax.ShapeDtypeStruct((fields, height, width), jnp.float32),
            jax.ShapeDtypeStruct((fields,), jnp.float32),
        ),
        in_specs=[vmem] * 4,
        out_specs=(vmem, vmem),
        compiler_params=params,
    )(sums, scaling, quotient, ocean_wet)


def solution(mesh):
    torus = Mesh(
        mesh.devices.reshape(mesh.shape["member"], 4, 2, mesh.shape["lon"]),
        ("member", "lat_0", "lat_1", "lon"),
    )
    in_specs = (
        P(MEMBER_LAT, "lon", None, None),
        P(MEMBER_LAT, "lon", None),
        P(MEMBER_LAT, "lon", None),
        P(MEMBER_LAT, "lon", None),
        P(MEMBER_LAT, "lon"),
        P(MEMBER_LAT, "lon"),
        P(MEMBER_LAT, "lon"),
        P(),
    )
    out_specs = (P(None, MEMBER_LAT, "lon"), P("member"))
    return jax.shard_map(body, mesh=torus, in_specs=in_specs, out_specs=out_specs, check_vma=False)
```

```python
import jax
import jax.numpy as jnp
from jax import lax
from jax.experimental import pallas as pl
from jax.experimental.pallas import tpu as pltpu
from jax.sharding import Mesh
from jax.sharding import PartitionSpec as P

MEMBER_LAT = ("member", "lat_0", "lat_1")
LAT = ("lat_0", "lat_1")

QUANTUM = 1024.0
LIMB_BITS = 16
LIMB_MASK = 65535
LANES = 128
VMEM_LIMIT = 16 * 1024 * 1024
SEND_VMEM_LIMIT = 62 * 1024 * 1024
PIECES = 4

TARGET, SOURCE, WET = 0, 16, 32
LOWER = 8


def units(values):
    return (values * QUANTUM).astype(jnp.int32)


def spread(per_lane, first):
    upper = jnp.sum((per_lane >> LIMB_BITS).astype(jnp.float32), axis=1, keepdims=True)
    lower = jnp.sum((per_lane & LIMB_MASK).astype(jnp.float32), axis=1, keepdims=True)
    lane = lax.broadcasted_iota(jnp.int32, per_lane.shape, 1)
    row = lax.broadcasted_iota(jnp.int32, per_lane.shape, 0)
    placed = jnp.where(lane == row + first, upper, 0.0) + jnp.where(lane == row + first + LOWER, lower, 0.0)
    return jnp.sum(placed, axis=0, keepdims=True).astype(jnp.int32)


def send_kernel(route, flux, frac, mask, area, chunks, route_s, flux_v, frac_v, mask_v, area_v, taken, in_sems):
    blocks, fields, cells = flux_v.shape
    tiles = taken.shape[0]
    band = cells // LANES
    block_rows = band * fields
    chunk_rows = chunks.shape[0] // tiles
    route_in = pltpu.make_async_copy(route.at[0], route_s, in_sems.at[0])
    frac_in = pltpu.make_async_copy(frac.at[0], frac_v, in_sems.at[1])
    mask_in = pltpu.make_async_copy(mask.at[0], mask_v, in_sems.at[2])
    area_in = pltpu.make_async_copy(area.at[0], area_v, in_sems.at[3])
    piece = blocks // PIECES
    flux_in = []
    for p in range(PIECES):
        part = pl.ds(p * piece, piece)
        flux_in.append(pltpu.make_async_copy(flux.at[0, part], flux_v.at[part], in_sems.at[4 + p]))
    for copy in [route_in, frac_in, mask_in, area_in] + flux_in:
        copy.start()
    lane = lax.broadcasted_iota(jnp.int32, (1, LANES), 1)
    nobody = jnp.full((1, LANES), float(blocks), jnp.float32)
    for tile in range(tiles):
        taken[tile] = 0
        chunks[tile * chunk_rows + chunk_rows - 1 : (tile + 1) * chunk_rows, :] = nobody
    route_in.wait()
    frac_in.wait()
    mask_in.wait()
    area_in.wait()
    amount = area_v[...] * frac_v[...] * mask_v[...].astype(jnp.float32)
    for b in range(blocks):
        if b % piece == 0:
            flux_in[b // piece].wait()
        target = route_s[b]
        tile = target // blocks
        order = taken[tile]
        taken[tile] = order + 1
        chunk = ((tile + (tiles - tiles // 2)) % tiles) * chunk_rows
        carried = flux_v[b] * amount[b : b + 1]
        first = chunk + order * block_rows
        for r in range(band):
            chunks[pl.ds(first + r * fields, fields), :] = carried[:, r * LANES : (r + 1) * LANES]
        last = pl.ds(chunk + chunk_rows - 1, 1)
        row = jnp.full((1, LANES), target % blocks, jnp.int32).astype(jnp.float32)
        chunks[last, :] = jnp.where(lane == order, row, chunks[last, :])


def beside_kernel(exponent, flux, frac, mask, area, ocean_area, ocean_wet, sums, scaling):
    amount = area[0] * frac[0] * mask[0].astype(jnp.float32)
    total = jnp.zeros(flux.shape[2:], jnp.int32)
    for b in range(flux.shape[1]):
        total = total + units(flux[0, b] * amount[b : b + 1])
    per_lane = total[:, :LANES]
    for at in range(LANES, total.shape[1], LANES):
        per_lane = per_lane + total[:, at : at + LANES]
    wet = jnp.sum(units(ocean_area[...] * ocean_wet[...].astype(jnp.float32)), axis=0, keepdims=True)
    sums[...] = spread(per_lane, SOURCE) + spread(wet, WET)
    lane = lax.broadcasted_iota(jnp.int32, (1, LANES), 1)
    scales = jnp.ones((1, LANES), jnp.int32)
    for f in range(flux.shape[2]):
        scales = jnp.where(lane == f, jnp.left_shift(jnp.int32(1), exponent[f]), scales)
    scaling[...] = scales.astype(jnp.float32)


def place_kernel(received, sent_sums, ocean_area, ocean_wet, quotient, sums, mapped):
    fields, height, width = quotient.shape
    stride = mapped.shape[0] // fields
    tiles = sums.shape[0]
    band = received.shape[0] // tiles // (2 * fields)
    chunk_rows = received.shape[0] // tiles
    for tile in range(tiles):
        chunk = tile * chunk_rows
        for order in range(2):
            row = received[chunk + chunk_rows - 1, order].astype(jnp.int32)
            for r in range(band):
                first = chunk + (order * band + r) * fields
                mapped[pl.ds(row * band + r, fields, stride), :] = received[first : first + fields, :]
    cover = ocean_wet[...].astype(jnp.float32)
    per_field = []
    for f in range(fields):
        field = mapped[f * stride : f * stride + height, :]
        per_field.append(jnp.sum(units(cover * field), axis=0, keepdims=True))
        quotient[f] = field / ocean_area[...]
    own = sent_sums[...] + spread(jnp.concatenate(per_field, axis=0), TARGET)
    for tile in range(sums.shape[0]):
        sums[tile] = own


def correct_kernel(sums, scaling, quotient, ocean_wet, flux, source_total):
    fields = quotient.shape[0]
    whole = sums[0]
    for tile in range(1, sums.shape[0]):
        whole = whole + sums[tile]
    upper = jnp.broadcast_to(whole, (8, LANES))
    lower = pltpu.roll(upper, LANES - LOWER, 1)
    upper = (upper + (lower >> LIMB_BITS)).astype(jnp.float32)
    integral = (upper * float(LIMB_MASK + 1) + (lower & LIMB_MASK).astype(jnp.float32)) * (1.0 / QUANTUM)
    source = pltpu.roll(integral, LANES - (SOURCE - TARGET), 1)
    lane = lax.broadcasted_iota(jnp.int32, (8, LANES), 1)
    row = lax.broadcasted_iota(jnp.int32, (8, LANES), 0)
    wet_area = jnp.sum(jnp.where(lane == WET, integral, 0.0), axis=1, keepdims=True)
    correction = (source - integral) / wet_area
    scales = jnp.broadcast_to(scaling[...], (8, LANES))
    per_field = jnp.sum(jnp.where(lane == row, correction, 0.0), axis=1, keepdims=True)
    scale = jnp.sum(jnp.where(lane == row, scales, 0.0), axis=1, keepdims=True)
    cover = ocean_wet[...].astype(jnp.float32)
    for f in range(fields):
        flux[f] = cover * scale[f : f + 1] * (quotient[f] + per_field[f : f + 1])
    source_total[...] = (source * scales)[0, :fields]


def exchange(chunks):
    tiles = lax.axis_size("lon")
    order = [(tiles // 2 + i) % tiles for i in range(tiles)]
    return lax.all_to_all(chunks, "lon", 0, 0, axis_index_groups=[order], tiled=True)


def body(ice_flux, ice_frac, ice_mask, ice_area, route, ocean_area, ocean_wet, exponent):
    blocks, fields, cells = ice_flux.shape[1:]
    height, width = ocean_area.shape
    tiles = lax.axis_size("lon")
    chunk_rows = 2 * fields * cells // LANES + 1
    vmem = pl.BlockSpec(memory_space=pltpu.VMEM)
    smem = pl.BlockSpec(memory_space=pltpu.SMEM)
    hbm = pl.BlockSpec(memory_space=pltpu.HBM)
    params = pltpu.CompilerParams(vmem_limit_bytes=VMEM_LIMIT)
    chunks = pl.pallas_call(
        send_kernel,
        out_shape=jax.ShapeDtypeStruct((tiles * chunk_rows, LANES), jnp.float32),
        in_specs=[hbm] * 5,
        out_specs=vmem,
        scratch_shapes=[
            pltpu.SMEM((blocks,), jnp.int32),
            pltpu.VMEM((blocks, fields, cells), jnp.float32),
            pltpu.VMEM((blocks, cells), jnp.float32),
            pltpu.VMEM((blocks, cells), jnp.int32),
            pltpu.VMEM((blocks, cells), jnp.float32),
            pltpu.SMEM((tiles,), jnp.int32),
            pltpu.SemaphoreType.DMA((4 + PIECES,)),
        ],
        compiler_params=pltpu.CompilerParams(vmem_limit_bytes=SEND_VMEM_LIMIT),
    )(route, ice_flux, ice_frac, ice_mask, ice_area)
    received = exchange(chunks.reshape(tiles, chunk_rows, 1, LANES)).reshape(tiles * chunk_rows, LANES)
    sums, scaling = pl.pallas_call(
        beside_kernel,
        out_shape=(
            jax.ShapeDtypeStruct((1, LANES), jnp.int32),
            jax.ShapeDtypeStruct((1, LANES), jnp.float32),
        ),
        in_specs=[smem] + [vmem] * 6,
        out_specs=(vmem, vmem),
        compiler_params=params,
    )(exponent, ice_flux, ice_frac, ice_mask, ice_area, ocean_area, ocean_wet)
    quotient, sums = pl.pallas_call(
        place_kernel,
        out_shape=(
            jax.ShapeDtypeStruct((fields, height, width), jnp.float32),
            jax.ShapeDtypeStruct((tiles, 1, LANES), jnp.int32),
        ),
        in_specs=[vmem] * 4,
        out_specs=(vmem, vmem),
        scratch_shapes=[pltpu.VMEM((fields * (height + 8), width), jnp.float32)],
        compiler_params=params,
    )(received, sums, ocean_area, ocean_wet)
    sums = exchange(lax.psum(sums, LAT))
    return pl.pallas_call(
        correct_kernel,
        out_shape=(
            jax.ShapeDtypeStruct((fields, height, width), jnp.float32),
            jax.ShapeDtypeStruct((fields,), jnp.float32),
        ),
        in_specs=[vmem] * 4,
        out_specs=(vmem, vmem),
        compiler_params=params,
    )(sums, scaling, quotient, ocean_wet)


def solution(mesh):
    torus = Mesh(
        mesh.devices.reshape(mesh.shape["member"], 4, 2, mesh.shape["lon"]),
        ("member", "lat_0", "lat_1", "lon"),
    )
    in_specs = (
        P(MEMBER_LAT, "lon", None, None),
        P(MEMBER_LAT, "lon", None),
        P(MEMBER_LAT, "lon", None),
        P(MEMBER_LAT, "lon", None),
        P(MEMBER_LAT, "lon"),
        P(MEMBER_LAT, "lon"),
        P(MEMBER_LAT, "lon"),
        P(),
    )
    out_specs = (P(None, MEMBER_LAT, "lon"), P("member"))
    return jax.shard_map(body, mesh=torus, in_specs=in_specs, out_specs=out_specs, check_vma=False)
```

```python
import functools

import jax
import jax.numpy as jnp
from jax import lax
from jax.experimental import pallas as pl
from jax.experimental.pallas import tpu as pltpu
from jax.sharding import Mesh
from jax.sharding import PartitionSpec as P

MEMBER_LAT = ("member", "lat_0", "lat_1")

QUANTUM = 1024.0
LIMB_BITS = 16
LIMB_MASK = 65535
LANES = 128
VMEM_LIMIT = 16 * 1024 * 1024
SEND_VMEM_LIMIT = 62 * 1024 * 1024
PIECES = 4

TARGET, SOURCE, WET = 0, 16, 32
LOWER = 8


def units(values):
    return (values * QUANTUM).astype(jnp.int32)


def spread(per_lane, first):
    upper = jnp.sum((per_lane >> LIMB_BITS).astype(jnp.float32), axis=1, keepdims=True)
    lower = jnp.sum((per_lane & LIMB_MASK).astype(jnp.float32), axis=1, keepdims=True)
    lane = lax.broadcasted_iota(jnp.int32, per_lane.shape, 1)
    row = lax.broadcasted_iota(jnp.int32, per_lane.shape, 0)
    placed = jnp.where(lane == row + first, upper, 0.0) + jnp.where(lane == row + first + LOWER, lower, 0.0)
    return jnp.sum(placed, axis=0, keepdims=True).astype(jnp.int32)


def send_kernel(route, flux, frac, mask, area, chunks, route_s, flux_v, frac_v, mask_v, area_v, taken, in_sems):
    blocks, fields, cells = flux_v.shape
    tiles = taken.shape[0]
    band = cells // LANES
    block_rows = band * fields
    chunk_rows = chunks.shape[0] // tiles
    route_in = pltpu.make_async_copy(route.at[0], route_s, in_sems.at[0])
    frac_in = pltpu.make_async_copy(frac.at[0], frac_v, in_sems.at[1])
    mask_in = pltpu.make_async_copy(mask.at[0], mask_v, in_sems.at[2])
    area_in = pltpu.make_async_copy(area.at[0], area_v, in_sems.at[3])
    piece = blocks // PIECES
    flux_in = []
    for p in range(PIECES):
        part = pl.ds(p * piece, piece)
        flux_in.append(pltpu.make_async_copy(flux.at[0, part], flux_v.at[part], in_sems.at[4 + p]))
    for copy in [route_in, frac_in, mask_in, area_in] + flux_in:
        copy.start()
    lane = lax.broadcasted_iota(jnp.int32, (1, LANES), 1)
    nobody = jnp.full((1, LANES), float(blocks), jnp.float32)
    for tile in range(tiles):
        taken[tile] = 0
        chunks[tile * chunk_rows : tile * chunk_rows + 1, :] = nobody
    route_in.wait()
    frac_in.wait()
    mask_in.wait()
    area_in.wait()
    amount = area_v[...] * frac_v[...] * mask_v[...].astype(jnp.float32)
    for b in range(blocks):
        if b % piece == 0:
            flux_in[b // piece].wait()
        target = route_s[b]
        tile = target // blocks
        order = taken[tile]
        taken[tile] = order + 1
        chunk = ((tile + (tiles - tiles // 2)) % tiles) * chunk_rows
        carried = flux_v[b] * amount[b : b + 1]
        first = chunk + 1 + order * block_rows
        for r in range(band):
            chunks[pl.ds(first + r * fields, fields), :] = carried[:, r * LANES : (r + 1) * LANES]
        head = pl.ds(chunk, 1)
        row = jnp.full((1, LANES), target % blocks, jnp.int32).astype(jnp.float32)
        chunks[head, :] = jnp.where(lane == order, row, chunks[head, :])


def beside_kernel(exponent, flux, frac, mask, area, ocean_area, ocean_wet, sums, scaling):
    amount = area[0] * frac[0] * mask[0].astype(jnp.float32)
    total = jnp.zeros(flux.shape[2:], jnp.int32)
    for b in range(flux.shape[1]):
        total = total + units(flux[0, b] * amount[b : b + 1])
    per_lane = total[:, :LANES]
    for at in range(LANES, total.shape[1], LANES):
        per_lane = per_lane + total[:, at : at + LANES]
    wet = jnp.sum(units(ocean_area[...] * ocean_wet[...].astype(jnp.float32)), axis=0, keepdims=True)
    sums[...] = spread(per_lane, SOURCE) + spread(wet, WET)
    lane = lax.broadcasted_iota(jnp.int32, (1, LANES), 1)
    scales = jnp.ones((1, LANES), jnp.int32)
    for f in range(flux.shape[2]):
        scales = jnp.where(lane == f, jnp.left_shift(jnp.int32(1), exponent[f]), scales)
    scaling[...] = scales.astype(jnp.float32)


def place_kernel(tiles, received, sent_sums, ocean_area, ocean_wet, quotient, sums, mapped):
    fields, height, width = quotient.shape
    stride = mapped.shape[0] // (fields + 1)
    band = received.shape[0] // tiles // (2 * fields)
    chunk_rows = received.shape[0] // tiles
    for tile in range(tiles):
        chunk = tile * chunk_rows
        for order in range(2):
            row = received[chunk, order].astype(jnp.int32)
            for r in range(band):
                first = chunk + 1 + (order * band + r) * fields
                mapped[pl.ds(row * band + r, fields, stride), :] = received[first : first + fields, :]
    cover = ocean_wet[...].astype(jnp.float32)
    per_field = []
    for f in range(fields):
        field = mapped[f * stride : f * stride + height, :]
        per_field.append(jnp.sum(units(cover * field), axis=0, keepdims=True))
        quotient[f] = field / ocean_area[...]
    sums[...] = sent_sums[...] + spread(jnp.concatenate(per_field, axis=0), TARGET)


def correct_kernel(sums, scaling, quotient, ocean_wet, flux, source_total):
    fields = quotient.shape[0]
    whole = sums[0]
    for tile in range(1, sums.shape[0]):
        whole = whole + sums[tile]
    upper = jnp.broadcast_to(whole, (8, LANES))
    lower = pltpu.roll(upper, LANES - LOWER, 1)
    upper = (upper + (lower >> LIMB_BITS)).astype(jnp.float32)
    integral = (upper * float(LIMB_MASK + 1) + (lower & LIMB_MASK).astype(jnp.float32)) * (1.0 / QUANTUM)
    source = pltpu.roll(integral, LANES - (SOURCE - TARGET), 1)
    lane = lax.broadcasted_iota(jnp.int32, (8, LANES), 1)
    row = lax.broadcasted_iota(jnp.int32, (8, LANES), 0)
    wet_area = jnp.sum(jnp.where(lane == WET, integral, 0.0), axis=1, keepdims=True)
    correction = (source - integral) / wet_area
    scales = jnp.broadcast_to(scaling[...], (8, LANES))
    per_field = jnp.sum(jnp.where(lane == row, correction, 0.0), axis=1, keepdims=True)
    scale = jnp.sum(jnp.where(lane == row, scales, 0.0), axis=1, keepdims=True)
    cover = ocean_wet[...].astype(jnp.float32)
    for f in range(fields):
        flux[f] = cover * scale[f : f + 1] * (quotient[f] + per_field[f : f + 1])
    source_total[...] = (source * scales)[0, :fields]


def exchange(chunks, rows=()):
    tiles = lax.axis_size("lon")
    order = [
        row * tiles + (tiles // 2 + i) % tiles for i in range(tiles) for row in range(chunks.shape[0] // tiles)
    ]
    return lax.all_to_all(chunks, rows + ("lon",), 0, 0, axis_index_groups=[order], tiled=True)


def body(ice_flux, ice_frac, ice_mask, ice_area, route, ocean_area, ocean_wet, exponent):
    blocks, fields, cells = ice_flux.shape[1:]
    height, width = ocean_area.shape
    tiles = lax.axis_size("lon")
    chunk_rows = 2 * fields * cells // LANES + 1
    vmem = pl.BlockSpec(memory_space=pltpu.VMEM)
    smem = pl.BlockSpec(memory_space=pltpu.SMEM)
    hbm = pl.BlockSpec(memory_space=pltpu.HBM)
    params = pltpu.CompilerParams(vmem_limit_bytes=VMEM_LIMIT)
    chunks = pl.pallas_call(
        send_kernel,
        out_shape=jax.ShapeDtypeStruct((tiles * chunk_rows, LANES), jnp.float32),
        in_specs=[hbm] * 5,
        out_specs=vmem,
        scratch_shapes=[
            pltpu.SMEM((blocks,), jnp.int32),
            pltpu.VMEM((blocks, fields, cells), jnp.float32),
            pltpu.VMEM((blocks, cells), jnp.float32),
            pltpu.VMEM((blocks, cells), jnp.int32),
            pltpu.VMEM((blocks, cells), jnp.float32),
            pltpu.SMEM((tiles,), jnp.int32),
            pltpu.SemaphoreType.DMA((4 + PIECES,)),
        ],
        compiler_params=pltpu.CompilerParams(vmem_limit_bytes=SEND_VMEM_LIMIT),
    )(route, ice_flux, ice_frac, ice_mask, ice_area)
    received = exchange(chunks.reshape(tiles, chunk_rows, 1, LANES)).reshape(tiles * chunk_rows, LANES)
    sums, scaling = pl.pallas_call(
        beside_kernel,
        out_shape=(
            jax.ShapeDtypeStruct((1, LANES), jnp.int32),
            jax.ShapeDtypeStruct((1, LANES), jnp.float32),
        ),
        in_specs=[smem] + [vmem] * 6,
        out_specs=(vmem, vmem),
        compiler_params=params,
    )(exponent, ice_flux, ice_frac, ice_mask, ice_area, ocean_area, ocean_wet)
    quotient, sums = pl.pallas_call(
        functools.partial(place_kernel, tiles),
        out_shape=(
            jax.ShapeDtypeStruct((fields, height, width), jnp.float32),
            jax.ShapeDtypeStruct((1, LANES), jnp.int32),
        ),
        in_specs=[vmem] * 4,
        out_specs=(vmem, vmem),
        scratch_shapes=[pltpu.VMEM(((fields + 1) * (height + 8), width), jnp.float32)],
        compiler_params=params,
    )(received, sums, ocean_area, ocean_wet)
    sums = lax.psum(sums, "lat_1")
    copies = lax.axis_size("lat_0") * tiles
    sums = exchange(jnp.broadcast_to(sums[None], (copies, 1, LANES)), ("lat_0",))
    return pl.pallas_call(
        correct_kernel,
        out_shape=(
            jax.ShapeDtypeStruct((fields, height, width), jnp.float32),
            jax.ShapeDtypeStruct((fields,), jnp.float32),
        ),
        in_specs=[vmem] * 4,
        out_specs=(vmem, vmem),
        compiler_params=params,
    )(sums, scaling, quotient, ocean_wet)


def solution(mesh):
    torus = Mesh(
        mesh.devices.reshape(mesh.shape["member"], 4, 2, mesh.shape["lon"]),
        ("member", "lat_0", "lat_1", "lon"),
    )
    in_specs = (
        P(MEMBER_LAT, "lon", None, None),
        P(MEMBER_LAT, "lon", None),
        P(MEMBER_LAT, "lon", None),
        P(MEMBER_LAT, "lon", None),
        P(MEMBER_LAT, "lon"),
        P(MEMBER_LAT, "lon"),
        P(MEMBER_LAT, "lon"),
        P(),
    )
    out_specs = (P(None, MEMBER_LAT, "lon"), P("member"))
    return jax.shard_map(body, mesh=torus, in_specs=in_specs, out_specs=out_specs, check_vma=False)
```

```python
import functools

import jax
import jax.numpy as jnp
from jax import lax
from jax.experimental import pallas as pl
from jax.experimental.pallas import tpu as pltpu
from jax.sharding import Mesh
from jax.sharding import PartitionSpec as P

MEMBER_LAT = ("member", "lat_0", "lat_1")

QUANTUM = 1024.0
LIMB_BITS = 16
LIMB_MASK = 65535
LANES = 128
VMEM_LIMIT = 16 * 1024 * 1024
SEND_VMEM_LIMIT = 62 * 1024 * 1024
PIECES = 4

TARGET, SOURCE, WET = 0, 16, 32
LOWER = 8


def units(values):
    return (values * QUANTUM).astype(jnp.int32)


def spread(per_lane, first):
    upper = jnp.sum((per_lane >> LIMB_BITS).astype(jnp.float32), axis=1, keepdims=True)
    lower = jnp.sum((per_lane & LIMB_MASK).astype(jnp.float32), axis=1, keepdims=True)
    lane = lax.broadcasted_iota(jnp.int32, per_lane.shape, 1)
    row = lax.broadcasted_iota(jnp.int32, per_lane.shape, 0)
    placed = jnp.where(lane == row + first, upper, 0.0) + jnp.where(lane == row + first + LOWER, lower, 0.0)
    return jnp.sum(placed, axis=0, keepdims=True).astype(jnp.int32)


def send_kernel(route, flux, frac, mask, area, chunks, route_s, flux_v, frac_v, mask_v, area_v, taken, in_sems):
    blocks, fields, cells = flux_v.shape
    tiles = taken.shape[0]
    band = cells // LANES
    block_rows = band * fields
    chunk_rows = chunks.shape[0] // tiles
    route_in = pltpu.make_async_copy(route.at[0], route_s, in_sems.at[0])
    frac_in = pltpu.make_async_copy(frac.at[0], frac_v, in_sems.at[1])
    mask_in = pltpu.make_async_copy(mask.at[0], mask_v, in_sems.at[2])
    area_in = pltpu.make_async_copy(area.at[0], area_v, in_sems.at[3])
    piece = blocks // PIECES
    flux_in = []
    for p in range(PIECES):
        part = pl.ds(p * piece, piece)
        flux_in.append(pltpu.make_async_copy(flux.at[0, part], flux_v.at[part], in_sems.at[4 + p]))
    for copy in [route_in, frac_in, mask_in, area_in] + flux_in:
        copy.start()
    lane = lax.broadcasted_iota(jnp.int32, (1, LANES), 1)
    nobody = jnp.full((1, LANES), float(blocks), jnp.float32)
    for tile in range(tiles):
        taken[tile] = 0
        chunks[tile * chunk_rows : tile * chunk_rows + 1, :] = nobody
    route_in.wait()
    frac_in.wait()
    mask_in.wait()
    area_in.wait()
    amount = area_v[...] * frac_v[...] * mask_v[...].astype(jnp.float32)
    for b in range(blocks):
        if b % piece == 0:
            flux_in[b // piece].wait()
        target = route_s[b]
        tile = target // blocks
        order = taken[tile]
        taken[tile] = order + 1
        chunk = ((tile + (tiles - ring_start(tiles))) % tiles) * chunk_rows
        carried = flux_v[b] * amount[b : b + 1]
        first = chunk + 1 + order * block_rows
        for r in range(band):
            chunks[pl.ds(first + r * fields, fields), :] = carried[:, r * LANES : (r + 1) * LANES]
        head = pl.ds(chunk, 1)
        row = jnp.full((1, LANES), target % blocks, jnp.int32).astype(jnp.float32)
        chunks[head, :] = jnp.where(lane == order, row, chunks[head, :])


def beside_kernel(exponent, flux, frac, mask, area, ocean_area, ocean_wet, sums, scaling):
    amount = area[0] * frac[0] * mask[0].astype(jnp.float32)
    total = jnp.zeros(flux.shape[2:], jnp.int32)
    for b in range(flux.shape[1]):
        total = total + units(flux[0, b] * amount[b : b + 1])
    per_lane = total[:, :LANES]
    for at in range(LANES, total.shape[1], LANES):
        per_lane = per_lane + total[:, at : at + LANES]
    wet = jnp.sum(units(ocean_area[...] * ocean_wet[...].astype(jnp.float32)), axis=0, keepdims=True)
    sums[...] = spread(per_lane, SOURCE) + spread(wet, WET)
    lane = lax.broadcasted_iota(jnp.int32, (1, LANES), 1)
    scales = jnp.ones((1, LANES), jnp.int32)
    for f in range(flux.shape[2]):
        scales = jnp.where(lane == f, jnp.left_shift(jnp.int32(1), exponent[f]), scales)
    scaling[...] = scales.astype(jnp.float32)


def place_kernel(tiles, received, sent_sums, ocean_area, ocean_wet, quotient, sums, mapped):
    fields, height, width = quotient.shape
    stride = mapped.shape[0] // (fields + 1)
    band = received.shape[0] // tiles // (2 * fields)
    chunk_rows = received.shape[0] // tiles
    for tile in range(tiles):
        chunk = tile * chunk_rows
        for order in range(2):
            row = received[chunk, order].astype(jnp.int32)
            for r in range(band):
                first = chunk + 1 + (order * band + r) * fields
                mapped[pl.ds(row * band + r, fields, stride), :] = received[first : first + fields, :]
    cover = ocean_wet[...].astype(jnp.float32)
    per_field = []
    for f in range(fields):
        field = mapped[f * stride : f * stride + height, :]
        per_field.append(jnp.sum(units(cover * field), axis=0, keepdims=True))
        quotient[f] = field / ocean_area[...]
    sums[...] = sent_sums[...] + spread(jnp.concatenate(per_field, axis=0), TARGET)


def correct_kernel(sums, scaling, quotient, ocean_wet, flux, source_total):
    fields = quotient.shape[0]
    whole = sums[0]
    for tile in range(1, sums.shape[0]):
        whole = whole + sums[tile]
    upper = jnp.broadcast_to(whole, (8, LANES))
    lower = pltpu.roll(upper, LANES - LOWER, 1)
    upper = (upper + (lower >> LIMB_BITS)).astype(jnp.float32)
    integral = (upper * float(LIMB_MASK + 1) + (lower & LIMB_MASK).astype(jnp.float32)) * (1.0 / QUANTUM)
    source = pltpu.roll(integral, LANES - (SOURCE - TARGET), 1)
    lane = lax.broadcasted_iota(jnp.int32, (8, LANES), 1)
    row = lax.broadcasted_iota(jnp.int32, (8, LANES), 0)
    wet_area = jnp.sum(jnp.where(lane == WET, integral, 0.0), axis=1, keepdims=True)
    correction = (source - integral) / wet_area
    scales = jnp.broadcast_to(scaling[...], (8, LANES))
    per_field = jnp.sum(jnp.where(lane == row, correction, 0.0), axis=1, keepdims=True)
    scale = jnp.sum(jnp.where(lane == row, scales, 0.0), axis=1, keepdims=True)
    cover = ocean_wet[...].astype(jnp.float32)
    for f in range(fields):
        flux[f] = cover * scale[f : f + 1] * (quotient[f] + per_field[f : f + 1])
    source_total[...] = (source * scales)[0, :fields]


def ring_start(tiles):
    return tiles * 5 // 8


def exchange(chunks):
    tiles = chunks.shape[0]
    order = [(ring_start(tiles) + i) % tiles for i in range(tiles)]
    return lax.all_to_all(chunks, "lon", 0, 0, axis_index_groups=[order], tiled=True)


def gathered(row):
    columns, tiles = lax.axis_size("lat_0"), lax.axis_size("lon")
    order = [
        (columns // 2 + j) % columns * tiles + (tiles // 2 + i) % tiles for i in range(tiles) for j in range(columns)
    ]
    copies = jnp.broadcast_to(row[None], (columns * tiles, *row.shape))
    return lax.all_to_all(copies, ("lat_0", "lon"), 0, 0, axis_index_groups=[order], tiled=True)


def body(ice_flux, ice_frac, ice_mask, ice_area, route, ocean_area, ocean_wet, exponent):
    blocks, fields, cells = ice_flux.shape[1:]
    height, width = ocean_area.shape
    tiles = lax.axis_size("lon")
    chunk_rows = 2 * fields * cells // LANES + 1
    vmem = pl.BlockSpec(memory_space=pltpu.VMEM)
    smem = pl.BlockSpec(memory_space=pltpu.SMEM)
    hbm = pl.BlockSpec(memory_space=pltpu.HBM)
    params = pltpu.CompilerParams(vmem_limit_bytes=VMEM_LIMIT)
    chunks = pl.pallas_call(
        send_kernel,
        out_shape=jax.ShapeDtypeStruct((tiles * chunk_rows, LANES), jnp.float32),
        in_specs=[hbm] * 5,
        out_specs=vmem,
        scratch_shapes=[
            pltpu.SMEM((blocks,), jnp.int32),
            pltpu.VMEM((blocks, fields, cells), jnp.float32),
            pltpu.VMEM((blocks, cells), jnp.float32),
            pltpu.VMEM((blocks, cells), jnp.int32),
            pltpu.VMEM((blocks, cells), jnp.float32),
            pltpu.SMEM((tiles,), jnp.int32),
            pltpu.SemaphoreType.DMA((4 + PIECES,)),
        ],
        compiler_params=pltpu.CompilerParams(vmem_limit_bytes=SEND_VMEM_LIMIT),
    )(route, ice_flux, ice_frac, ice_mask, ice_area)
    received = exchange(chunks.reshape(tiles, chunk_rows, 1, LANES)).reshape(tiles * chunk_rows, LANES)
    sums, scaling = pl.pallas_call(
        beside_kernel,
        out_shape=(
            jax.ShapeDtypeStruct((1, LANES), jnp.int32),
            jax.ShapeDtypeStruct((1, LANES), jnp.float32),
        ),
        in_specs=[smem] + [vmem] * 6,
        out_specs=(vmem, vmem),
        compiler_params=params,
    )(exponent, ice_flux, ice_frac, ice_mask, ice_area, ocean_area, ocean_wet)
    quotient, sums = pl.pallas_call(
        functools.partial(place_kernel, tiles),
        out_shape=(
            jax.ShapeDtypeStruct((fields, height, width), jnp.float32),
            jax.ShapeDtypeStruct((1, LANES), jnp.int32),
        ),
        in_specs=[vmem] * 4,
        out_specs=(vmem, vmem),
        scratch_shapes=[pltpu.VMEM(((fields + 1) * (height + 8), width), jnp.float32)],
        compiler_params=params,
    )(received, sums, ocean_area, ocean_wet)
    sums = gathered(lax.psum(sums, "lat_1"))
    return pl.pallas_call(
        correct_kernel,
        out_shape=(
            jax.ShapeDtypeStruct((fields, height, width), jnp.float32),
            jax.ShapeDtypeStruct((fields,), jnp.float32),
        ),
        in_specs=[vmem] * 4,
        out_specs=(vmem, vmem),
        compiler_params=params,
    )(sums, scaling, quotient, ocean_wet)


def solution(mesh):
    torus = Mesh(
        mesh.devices.reshape(mesh.shape["member"], 4, 2, mesh.shape["lon"]),
        ("member", "lat_0", "lat_1", "lon"),
    )
    in_specs = (
        P(MEMBER_LAT, "lon", None, None),
        P(MEMBER_LAT, "lon", None),
        P(MEMBER_LAT, "lon", None),
        P(MEMBER_LAT, "lon", None),
        P(MEMBER_LAT, "lon"),
        P(MEMBER_LAT, "lon"),
        P(MEMBER_LAT, "lon"),
        P(),
    )
    out_specs = (P(None, MEMBER_LAT, "lon"), P("member"))
    return jax.shard_map(body, mesh=torus, in_specs=in_specs, out_specs=out_specs, check_vma=False)
```
